256 devices in a mesh: row: 16 (over z_lo, y, core), col: 16 (over x, z_hi).
Axes of the slice: x: 4, y: 4, z: 8 (z_hi: 4, z_lo: 2; z = z_hi * 2 + z_lo), core: 2. Of those that a mesh axis runs over, the one named last changes fastest.
Arguments:
- block_input: bfloat16 [2048, 8192], P('col', 'row'), may hold values from -6 to 6
- out_grad: bfloat16 [2048, 8192], P('col', 'row'), may hold values from -6 to 6
- gate_pre: bfloat16 [2048, 14336], P('row', 'col'), may hold values from -8 to 8
- up_pre: bfloat16 [2048, 14336], P('row', 'col'), may hold values from -6 to 6
- gate_weight: bfloat16 [8192, 14336], P('row', 'col'), may hold values from -0.0625 to 0.0625
- up_weight: bfloat16 [8192, 14336], P('row', 'col'), may hold values from -0.0625 to 0.0625
- down_weight: bfloat16 [8192, 14336], P('row', 'col'), may hold values from -0.046875 to 0.046875
Outputs:
- input_grad: bfloat16 [2048, 8192], P('col', 'row')
- grad_gate: float32 [8192, 14336], P('row', 'col')
- grad_up: float32 [8192, 14336], P('row', 'col')
- grad_down: float32 [8192, 14336], P('row', 'col')
The draws below stay inside these ranges and needn't reach their ends.
All inputs are finite; a program needn't handle non-finite values.
Results may differ from the reference program's by a relative error of at most 0.0049.
Values may be sent and summed in bfloat16 or wider, within the bound.
A program may use at most 128 MiB of HBM per device.

```python
import jax
import jax.numpy as jnp
from jax import lax

D = 8192
FF = 14336
TOKENS = 2048


def steps_of(key, shape, split, smallest, largest):
    def one(dim, blocks):
        heights = jax.random.uniform(jax.random.fold_in(jax.random.fold_in(key, 6), dim), (blocks,), jnp.float32, smallest / len(split), largest / len(split))
        return jnp.repeat(jnp.exp(heights), shape[dim] // blocks).reshape((-1,) + (1,) * (len(shape) - dim - 1))

    factor_of = one(*split[0])
    for cut in split[1:]:
        factor_of = factor_of * one(*cut)
    return factor_of


def centred(key, dims, width, limit, split=(), dtype=jnp.bfloat16):
    result = width * jax.random.normal(key, dims, jnp.float32)
    if split:
        result = result * steps_of(key, dims, split, -0.22, 0.18)
    return jnp.clip(result, -limit, limit).astype(dtype)


def setup_inputs(seed: int = 0) -> dict:
    splits = jax.random.split(jax.random.key(seed), 8)
    return {
        "block_input": centred(splits[0], (TOKENS, D), 1.0, 6.0, ((0, 16), (1, 16))),
        "out_grad": centred(splits[1], (TOKENS, D), 1.0, 6.0, ((0, 16), (1, 16))),
        "gate_pre": centred(splits[2], (TOKENS, FF), 1.5, 8.0, ((0, 16), (1, 16))),
        "up_pre": centred(splits[3], (TOKENS, FF), 1.0, 6.0, ((0, 16), (1, 16))),
        "gate_weight": centred(splits[4], (D, FF), D ** -0.5, 0.0625, ((0, 16), (1, 16))),
        "up_weight": centred(splits[5], (D, FF), D ** -0.5, 0.0625, ((0, 16), (1, 16))),
        "down_weight": centred(splits[6], (D, FF), FF ** -0.5, 0.046875, ((0, 16), (1, 16))),
    }


def reference(block_input, out_grad, gate_pre, up_pre, gate_weight, up_weight, down_weight):
    hidden_grad = jnp.dot(out_grad, down_weight, preferred_element_type=jnp.float32)
    gate_f = gate_pre.astype(jnp.float32)
    up_f = up_pre.astype(jnp.float32)
    sig = jax.nn.sigmoid(gate_f)
    hidden = (gate_f * sig * up_f).astype(jnp.bfloat16)
    up_delta = (hidden_grad * gate_f * sig).astype(jnp.bfloat16)
    gate_delta = (hidden_grad * up_f * sig * (1.0 + gate_f * (1.0 - sig))).astype(jnp.bfloat16)
    contract = (((0,), (0,)), ((), ()))
    grad_down = lax.dot_general(out_grad, hidden, contract, preferred_element_type=jnp.float32)
    grad_gate = lax.dot_general(block_input, gate_delta, contract, preferred_element_type=jnp.float32)
    grad_up = lax.dot_general(block_input, up_delta, contract, preferred_element_type=jnp.float32)
    inner = (((1,), (1,)), ((), ()))
    input_grad = lax.dot_general(gate_delta, gate_weight, inner, preferred_element_type=jnp.float32)
    input_grad = input_grad + lax.dot_general(up_delta, up_weight, inner, preferred_element_type=jnp.float32)
    return input_grad.astype(jnp.bfloat16), grad_gate, grad_up, grad_down
```

```python
import jax
import jax.numpy as jnp
from jax import lax
from jax.experimental import pallas as pl
from jax.experimental.pallas import tpu as pltpu
from jax.sharding import PartitionSpec as P

MESH = pl.DeviceIdType.MESH
BF = jnp.bfloat16
F32 = jnp.float32
T, D, F = 128, 512, 896
Q = 32


def dot(a, b):
    return jnp.dot(a, b, preferred_element_type=F32)


def dot_nt(a, b):
    return lax.dot_general(a, b, (((1,), (1,)), ((), ())), preferred_element_type=F32)


def dot_tn(a, b):
    return lax.dot_general(a, b, (((0,), (0,)), ((), ())), preferred_element_type=F32)


def kernel(
    x_in, g_in, gate_in, up_in, wg_in, wu_in, wd_in,
    ig_out, gg_out, gu_out, gd_out,
    GF, GS, XF, GA, UP, HP, HR, HO, HZS, HZR, HG, HID, DG, DU,
    IPO, IPS, IPR, IZS, IZR, WD, WDS, WG, WU, OUT, IGO,
    lsem, osem, bs, br, xs, xr, rs, rr, ss, sr,
):
    row = lax.axis_index("row")
    col = lax.axis_index("col")
    zl, y, k = row // 8, (row // 2) % 4, row % 2
    x, zh = col // 4, col % 4

    def at(dzl=0, dy=0, dk=0, dx=0, dzh=0):
        r = ((zl + dzl) % 2) * 8 + ((y + dy) % 4) * 2 + (k + dk) % 2
        c = ((x + dx) % 4) * 4 + (zh + dzh) % 4
        return {"row": r, "col": c}

    started = []

    def send(src, dst, send_sem, recv_sem, dev):
        cp = pltpu.make_async_remote_copy(
            src_ref=src, dst_ref=dst, send_sem=send_sem, recv_sem=recv_sem, device_id=dev, device_id_type=MESH
        )
        cp.start()
        started.append(cp)

    def arrived(dst, recv_sem):
        pltpu.make_async_copy(dst, dst, recv_sem).wait()

    peers = [at(dk=1), at(dzl=1)]
    for d in (1, 2, 3):
        peers += [at(dy=d), at(dx=d), at(dzh=d)]
    barrier = pltpu.get_barrier_semaphore()
    for p in peers:
        pl.semaphore_signal(barrier, inc=1, device_id=p, device_id_type=MESH)
    pl.semaphore_wait(barrier, len(peers))

    def blk(xx, zz):
        xx, zz = (xx + 8) % 4, (zz + 8) % 4
        return zz % 2, 2 * xx + zz // 2

    myp, myh = blk(x, zh)
    mine = 4 * zl + y
    other = 4 * (1 - zl) + y

    for e in (1, 3, 2):
        send(g_in, GF.at[myp, myh], bs.at[0, e, 0], br.at[0, e, 0], at(dzh=e))
    for d in (1, 3, 2):
        send(g_in, GF.at[myp, myh], bs.at[0, 0, d], br.at[0, 0, d], at(dx=d))
    loads = []
    for i, (src, dst) in enumerate(
        [
            (g_in, GF.at[myp, myh]), (wd_in, WD), (gate_in, GA.at[mine]), (up_in, UP.at[mine]),
            (x_in, XF.at[myp, myh]), (wg_in, WG), (wu_in, WU),
        ]
    ):
        cp = pltpu.make_async_copy(src, dst, lsem.at[i])
        cp.start()
        loads.append(cp)
    send(wd_in, WDS, ss.at[0], sr.at[0], at(dk=1))

    for d in (1, 3, 2):
        send(gate_in, GA.at[mine], rs.at[0, d], rr.at[0, d], at(dy=d))
        send(up_in, UP.at[mine], rs.at[1, d], rr.at[1, d], at(dy=d))
    send(gate_in, GA.at[mine], rs.at[0, 0], rr.at[0, 0], at(dzl=1))
    send(up_in, UP.at[mine], rs.at[1, 0], rr.at[1, 0], at(dzl=1))

    def forward_x(buf, i):
        for e in (1, 3, 2):
            p, h = blk(x, zh - e)
            arrived(buf.at[p, h], br.at[i, e, 0])
            for d in (1, 3, 2):
                send(buf.at[p, h], buf.at[p, h], bs.at[i, e, d], br.at[i, e, d], at(dx=d))

    def wait_x(buf, i, d):
        for e in range(4):
            p, h = blk(x - d, zh - e)
            arrived(buf.at[p, h], br.at[i, e, d])

    forward_x(GF, 0)

    for e in (1, 3, 2):
        send(x_in, XF.at[myp, myh], bs.at[1, e, 0], br.at[1, e, 0], at(dzh=e))

    arrived(GA.at[other], rr.at[0, 0])
    for d in (1, 3, 2):
        send(GA.at[other], GA.at[other], rs.at[0, 4 + d], rr.at[0, 4 + d], at(dy=d))
    for d in (1, 3, 2):
        h = 4 * zl + (y + 4 - d) % 4
        arrived(UP.at[h], rr.at[1, d])
        send(UP.at[h], UP.at[h], rs.at[1, 4 + d], rr.at[1, 4 + d], at(dzl=1))

    loads[0].wait()
    loads[1].wait()

    order = (1, 3, 2, 0)

    def base(n):
        return 2 * ((x + 4 - order[n]) % 4)

    def to_sibling(n):
        if order[n]:
            wait_x(GF, 0, order[n])
        b = base(n)
        send(GF.at[1 - k, pl.ds(b, 2)], GS.at[pl.ds(b, 2)], ss.at[1 + n], sr.at[1 + n], at(dk=1))

    def stage_a(n):
        b = base(n)
        arrived(GS.at[pl.ds(b, 2)], sr.at[1 + n])
        if n == 0:
            arrived(WDS, sr.at[0])
        part = dot(GF[k, pl.ds(b, 2)].reshape(2 * T, D), WD[...])
        part = part + dot(GS[pl.ds(b, 2)].reshape(2 * T, D), WDS[...])
        part = part.astype(BF).reshape(2, 4, Q, F)
        for yy in range(4):
            HP[n, yy] = part[:, yy]
        for d in (1, 3, 2):
            send(HP.at[n, (y + d) % 4], HR.at[n, d - 1], xs.at[n, d], xr.at[n, d], at(dy=d))

    def stage_b(n):
        for d in (1, 3, 2):
            arrived(HR.at[n, d - 1], xr.at[n, d])

        def total(z):
            t = HP[n, y, z].astype(F32)
            for d in range(3):
                t = t + HR[n, d, z].astype(F32)
            return t

        HZS[n] = total(1 - zl)
        send(HZS.at[n], HZR.at[n], xs.at[n, 0], xr.at[n, 0], at(dzl=1))
        HO[n] = total(zl)

    def stage_c(n):
        b = base(n)
        arrived(HZR.at[n], xr.at[n, 0])
        HG[b + zl, y] = (HO[n] + HZR[n]).astype(BF)
        own = HG.at[b + zl, y]
        send(own, own, xs.at[n, 4], xr.at[n, 4], at(dzl=1))
        for d in (1, 3, 2):
            send(own, own, xs.at[n, 4 + d], xr.at[n, 4 + d], at(dy=d))

    def stage_d(n):
        b = base(n)
        theirs = HG.at[b + 1 - zl, y]
        arrived(theirs, xr.at[n, 4])
        for d in (1, 3, 2):
            send(theirs, theirs, xs.at[n, 8 + d], xr.at[n, 8 + d], at(dy=d))

    def stage_e(n):
        b = base(n)
        for d in (1, 3, 2):
            yy = (y + 4 - d) % 4
            arrived(HG.at[b + zl, yy], xr.at[n, 4 + d])
            arrived(HG.at[b + 1 - zl, yy], xr.at[n, 8 + d])
        if n == 0:
            loads[2].wait()
            loads[3].wait()
            for d in (1, 3, 2):
                yy = (y + 4 - d) % 4
                arrived(GA.at[4 * zl + yy], rr.at[0, d])
                arrived(GA.at[4 * (1 - zl) + yy], rr.at[0, 4 + d])
                arrived(UP.at[4 * (1 - zl) + yy], rr.at[1, 4 + d])
            arrived(UP.at[other], rr.at[1, 0])

        def tile(t, _):
            i, j = b + t // 8, t % 8
            rows = pl.ds(pl.multiple_of(j * 16, 16), 16)
            hg = HG[i, j // 2, pl.ds(pl.multiple_of((j % 2) * 16, 16), 16), :].astype(F32)
            ga = GA[i, rows, :].astype(F32)
            up = UP[i, rows, :].astype(F32)
            sig = jax.nn.sigmoid(ga)
            gs = ga * sig
            HID[k, i, rows, :] = (gs * up).astype(BF)
            DU[k, i, rows, :] = (hg * gs).astype(BF)
            DG[k, i, rows, :] = (hg * up * sig * (1.0 + ga * (1.0 - sig))).astype(BF)
            return 0

        lax.fori_loop(0, 16, tile, 0)
        for j, buf in enumerate((DG, DU, HID)):
            part = buf.at[k, pl.ds(b, 2)]
            send(part, part, ss.at[5 + 3 * n + j], sr.at[5 + 3 * n + j], at(dk=1))

    def stage_f(n):
        b = base(n)
        if n == 0:
            loads[5].wait()
            loads[6].wait()
        for p in range(2):
            if p == 0:
                for j, buf in enumerate((DG, DU)):
                    arrived(buf.at[1 - k, pl.ds(b, 2)], sr.at[5 + 3 * n + j])
            part = dot_nt(DG[p, pl.ds(b, 2)].reshape(2 * T, F), WG[...])
            part = part + dot_nt(DU[p, pl.ds(b, 2)].reshape(2 * T, F), WU[...])
            part = part.reshape(2, T, D)
            if order[n]:
                IPS[n, p] = part.astype(BF)
            else:
                IPO[p] = part
        if order[n]:
            send(IPS.at[n], IPR.at[n], xs.at[n, 12], xr.at[n, 12], at(dx=4 - order[n]))

    to_sibling(3)
    to_sibling(0)
    stage_a(0)
    for d in (1, 3, 2):
        send(x_in, XF.at[myp, myh], bs.at[1, 0, d], br.at[1, 0, d], at(dx=d))
    to_sibling(1)
    stage_a(1)
    stage_b(0)
    to_sibling(2)
    stage_a(2)
    stage_b(1)
    stage_c(0)
    forward_x(XF, 1)
    stage_a(3)
    stage_b(2)
    stage_c(1)
    stage_d(0)
    stage_b(3)
    stage_c(2)
    stage_d(1)
    stage_e(0)
    stage_c(3)
    stage_d(2)
    stage_f(0)
    stage_e(1)
    stage_d(3)
    stage_f(1)
    stage_e(2)
    stage_f(2)
    stage_e(3)
    stage_f(3)

    for n in range(3):
        arrived(IPR.at[n], xr.at[n, 12])
    for p in range(2):
        for i in range(2):
            t = IPO[p, i]
            for n in range(3):
                t = t + IPR[n, p, i].astype(F32)
            IZS[p, i] = t.astype(BF)
            IPO[p, i] = t
    for e in (2, 1, 3):
        zz = (zh + e) % 4
        send(IZS.at[zz % 2, zz // 2], IZR.at[e - 1], rs.at[2, e], rr.at[2, e], at(dzh=e))

    for n in range(4):
        b = base(n)
        arrived(HID.at[1 - k, pl.ds(b, 2)], sr.at[5 + 3 * n + 2])
    outs = []

    def weight_grad(i, lhs, rhs, out):
        a = lhs[...].reshape(16 * T, D)

        def cols(j, _):
            c = pl.ds(pl.multiple_of(j * 128, 128), 128)
            OUT[i, :, c] = dot_tn(a, rhs[:, :, :, c].reshape(16 * T, 128))
            return 0

        lax.fori_loop(0, F // 128, cols, 0)
        cp = pltpu.make_async_copy(OUT.at[i], out, osem.at[i])
        cp.start()
        outs.append(cp)

    weight_grad(0, GF, HID, gd_out)
    loads[4].wait()
    for d in (1, 3, 2):
        wait_x(XF, 1, d)
    weight_grad(1, XF, DG, gg_out)
    weight_grad(2, XF, DU, gu_out)

    t = IPO[myp, zh // 2]
    for e in (1, 2, 3):
        arrived(IZR.at[e - 1], rr.at[2, e])
        t = t + IZR[e - 1].astype(F32)
    IGO[...] = t.astype(BF)
    cp = pltpu.make_async_copy(IGO, ig_out, osem.at[3])
    cp.start()
    outs.append(cp)
    for cp in outs:
        cp.wait()
    for cp in started:
        cp.wait_send()


def body(*args):
    any_spec = pl.BlockSpec(memory_space=pl.ANY)
    dma = pltpu.SemaphoreType.DMA
    return pl.pallas_call(
        kernel,
        out_shape=[
            jax.ShapeDtypeStruct((T, D), BF),
            jax.ShapeDtypeStruct((D, F), F32),
            jax.ShapeDtypeStruct((D, F), F32),
            jax.ShapeDtypeStruct((D, F), F32),
        ],
        in_specs=[any_spec] * 7,
        out_specs=[any_spec] * 4,
        scratch_shapes=[
            pltpu.VMEM((2, 8, T, D), BF),
            pltpu.VMEM((8, T, D), BF),
            pltpu.VMEM((2, 8, T, D), BF),
            pltpu.VMEM((8, T, F), BF),
            pltpu.VMEM((8, T, F), BF),
            pltpu.VMEM((4, 4, 2, Q, F), BF),
            pltpu.VMEM((4, 3, 2, Q, F), BF),
            pltpu.VMEM((4, Q, F), F32),
            pltpu.VMEM((4, Q, F), F32),
            pltpu.VMEM((4, Q, F), F32),
            pltpu.VMEM((8, 4, Q, F), BF),
            pltpu.VMEM((2, 8, T, F), BF),
            pltpu.VMEM((2, 8, T, F), BF),
            pltpu.VMEM((2, 8, T, F), BF),
            pltpu.VMEM((2, 2, T, D), F32),
            pltpu.VMEM((3, 2, 2, T, D), BF),
            pltpu.VMEM((3, 2, 2, T, D), BF),
            pltpu.VMEM((2, 2, T, D), BF),
            pltpu.VMEM((3, T, D), BF),
            pltpu.VMEM((D, F), BF),
            pltpu.VMEM((D, F), BF),
            pltpu.VMEM((D, F), BF),
            pltpu.VMEM((D, F), BF),
            pltpu.VMEM((3, D, F), F32),
            pltpu.VMEM((T, D), BF),
            dma((7,)),
            dma((4,)),
            dma((2, 4, 4)),
            dma((2, 4, 4)),
            dma((4, 13)),
            dma((4, 13)),
            dma((3, 8)),
            dma((3, 8)),
            dma((17,)),
            dma((17,)),
        ],
        compiler_params=pltpu.CompilerParams(
            collective_id=0, has_side_effects=True, vmem_limit_bytes=56 * 1024 * 1024
        ),
        cost_estimate=pl.CostEstimate(flops=12 * 2048 * D * F, bytes_accessed=10 << 20, transcendentals=0),
        name="swiglu_backward",
    )(*args)


def solution(mesh):
    return jax.shard_map(
        body,
        mesh=mesh,
        in_specs=(
            P("col", "row"),
            P("col", "row"),
            P("row", "col"),
            P("row", "col"),
            P("row", "col"),
            P("row", "col"),
            P("row", "col"),
        ),
        out_specs=(P("col", "row"), P("row", "col"), P("row", "col"), P("row", "col")),
        check_vma=False,
    )
```

```python
import jax
import jax.numpy as jnp
from jax import lax
from jax.experimental import pallas as pl
from jax.experimental.pallas import tpu as pltpu
from jax.sharding import PartitionSpec as P

MESH = pl.DeviceIdType.MESH
BF = jnp.bfloat16
F32 = jnp.float32
T, D, F = 128, 512, 896
Q = 32
ZSUM = (0, 1, 1, 0)
ZGATHER = (1, 0, 1, 0)


def dot(a, b):
    return jnp.dot(a, b, preferred_element_type=F32)


def dot_nt(a, b):
    return lax.dot_general(a, b, (((1,), (1,)), ((), ())), preferred_element_type=F32)


def dot_tn(a, b):
    return lax.dot_general(a, b, (((0,), (0,)), ((), ())), preferred_element_type=F32)


def kernel(
    x_in, g_in, gate_in, up_in, wg_in, wu_in, wd_in,
    ig_out, gg_out, gu_out, gd_out,
    GF, GS, XF, GA, UP, FU, FG, HP, HF, HR, HZS, HZR, HG, HID, DG, DU,
    IPO, IPS, IPR, IZ2, IXS, IXR, IZS, IZR, WD, WDS, WG, WU, OUT, IGO,
    lsem, osem, bs, br, xs, xr, rs, rr, ss, sr,
):
    row = lax.axis_index("row")
    col = lax.axis_index("col")
    zl, y, k = row // 8, (row // 2) % 4, row % 2
    x, zh = col // 4, col % 4

    def at(dzl=0, dy=0, dk=0, dx=0, dzh=0):
        r = ((zl + dzl) % 2) * 8 + ((y + dy) % 4) * 2 + (k + dk) % 2
        c = ((x + dx) % 4) * 4 + (zh + dzh) % 4
        return {"row": r, "col": c}

    started = []

    def send(src, dst, send_sem, recv_sem, dev):
        cp = pltpu.make_async_remote_copy(
            src_ref=src, dst_ref=dst, send_sem=send_sem, recv_sem=recv_sem, device_id=dev, device_id_type=MESH
        )
        cp.start()
        started.append(cp)

    def arrived(dst, recv_sem):
        pltpu.make_async_copy(dst, dst, recv_sem).wait()

    def blk(xx, zz):
        xx, zz = (xx + 8) % 4, (zz + 8) % 4
        return zz % 2, 2 * xx + zz // 2

    myp, myh = blk(x, zh)
    mine = 4 * zl + y
    other = 4 * (1 - zl) + y

    loads = []
    for i, (src, dst) in enumerate(
        [
            (g_in, GF.at[myp, myh]), (wd_in, WD), (gate_in, GA.at[mine]), (up_in, UP.at[mine]),
            (x_in, XF.at[myp, myh]), (wg_in, WG), (wu_in, WU),
        ]
    ):
        cp = pltpu.make_async_copy(src, dst, lsem.at[i])
        cp.start()
        loads.append(cp)

    peers = [at(dk=1), at(dzl=1)]
    for d in (1, 2, 3):
        peers += [at(dy=d), at(dx=d), at(dzh=d)]
    barrier = pltpu.get_barrier_semaphore()
    for p in peers:
        pl.semaphore_signal(barrier, inc=1, device_id=p, device_id_type=MESH)
    pl.semaphore_wait(barrier, len(peers))

    for e in (1, 3):
        send(g_in, GF.at[myp, myh], bs.at[0, e, 0], br.at[0, e, 0], at(dzh=e))
    for d in (1, 3):
        send(g_in, GF.at[myp, myh], bs.at[0, 0, d], br.at[0, 0, d], at(dx=d))
    for i, src, buf in ((0, gate_in, GA), (1, up_in, UP)):
        for d in (1, 3):
            send(src, buf.at[mine], rs.at[i, d], rr.at[i, d], at(dy=d))
    send(wd_in, WDS, ss.at[0], sr.at[0], at(dk=1))

    HALF = (pl.ds(0, T // 2), pl.ds(T // 2, T // 2))

    def forward_z(buf, i, e):
        p, h = blk(x, zh - e)
        if e == 2:
            for j in range(2):
                arrived(buf.at[p, h, HALF[j]], br.at[i, 2, 5 * j])
        else:
            arrived(buf.at[p, h], br.at[i, e, 0])
            half = buf.at[p, h, HALF[e // 2]]
            send(half, half, bs.at[i, 2, 5 * (e // 2)], br.at[i, 2, 5 * (e // 2)], at(dzh=e))
        for d in (1, 3):
            send(buf.at[p, h], buf.at[p, h], bs.at[i, e, d], br.at[i, e, d], at(dx=d))

    def forward_x(buf, i, e):
        for j, d in enumerate((1, 3)):
            p, h = blk(x - d, zh - e)
            arrived(buf.at[p, h], br.at[i, e, d])
            half = buf.at[p, h, HALF[j]]
            send(half, half, bs.at[i, e, 2 + 2 * j], br.at[i, e, 2 + 2 * j], at(dx=d))

    def wait_x(buf, i, d):
        if d == 2:
            for e in range(4):
                p, h = blk(x - 2, zh - e)
                for j in range(2):
                    arrived(buf.at[p, h, HALF[j]], br.at[i, e, 2 + 2 * j])

    def forward_y(i, buf, z, o):
        for j, d in enumerate((1, 3)):
            h = 4 * z + (y + 4 - d) % 4
            arrived(buf.at[h], rr.at[i, o + d])
            half = buf.at[h, HALF[j]]
            send(half, half, rs.at[i, o + 2 + 2 * j], rr.at[i, o + 2 + 2 * j], at(dy=d))

    def wait_y(i, buf, z, o):
        for j in range(2):
            arrived(buf.at[4 * z + (y + 2) % 4, HALF[j]], rr.at[i, o + 2 + 2 * j])

    def forward_zl(i, buf):
        arrived(buf.at[other], rr.at[i, 0])
        for d in (1, 3):
            send(buf.at[other], buf.at[other], rs.at[i, 5 + d], rr.at[i, 5 + d], at(dy=d))

    order = (1, 3, 2, 0)

    def base(n):
        return 2 * ((x + 4 - order[n]) % 4)

    def to_sibling(n):
        if order[n]:
            wait_x(GF, 0, order[n])
        else:
            loads[0].wait()
        b = base(n)
        send(GF.at[1 - k, pl.ds(b, 2)], GS.at[pl.ds(b, 2)], ss.at[1 + n], sr.at[1 + n], at(dk=1))

    def stage_a(n):
        b = base(n)
        arrived(GS.at[pl.ds(b, 2)], sr.at[1 + n])
        if n == 3:
            loads[1].wait()
            arrived(WDS, sr.at[0])
        part = dot(GF[k, pl.ds(b, 2)].reshape(2 * T, D), WD[...])
        part = (part + dot(GS[pl.ds(b, 2)].reshape(2 * T, D), WDS[...])).reshape(2, 4, Q, F)
        if ZSUM[n]:
            part = part.reshape(8, Q, F)
            HF[n] = part
            HP[n] = part.astype(BF)
            send(HP.at[n, pl.ds(4 * (1 - zl), 4)], HR.at[n, pl.ds(0, 4)], xs.at[n, 0], xr.at[n, 0], at(dzl=1))
        else:
            for yy in range(4):
                HF[n, 2 * yy : 2 * yy + 2] = part[:, yy]
                HP[n, 2 * yy : 2 * yy + 2] = part[:, yy].astype(BF)
            for d in (1, 3, 2):
                to = 2 * ((y + d) % 4)
                send(HP.at[n, pl.ds(to, 2)], HR.at[n, pl.ds(2 * d - 2, 2)], xs.at[n, d], xr.at[n, d], at(dy=d))

    def stage_b(n):
        if ZSUM[n]:
            arrived(HR.at[n, pl.ds(0, 4)], xr.at[n, 0])
            for yy in range(4):
                t = HF[n, 4 * zl + yy] + HR[n, yy].astype(F32)
                HF[n, 4 * zl + yy] = t
                HP[n, 4 * zl + yy] = t.astype(BF)
            for d in (1, 3, 2):
                to = 4 * zl + (y + d) % 4
                send(HP.at[n, to], HR.at[n, 3 + d], xs.at[n, d], xr.at[n, d], at(dy=d))
        else:
            for d in (1, 3, 2):
                arrived(HR.at[n, pl.ds(2 * d - 2, 2)], xr.at[n, d])

            def total(z):
                t = HF[n, 2 * y + z]
                for d in (1, 2, 3):
                    t = t + HR[n, 2 * d - 2 + z].astype(F32)
                return t

            HZS[n] = total(1 - zl)
            send(HZS.at[n], HZR.at[n], xs.at[n, 0], xr.at[n, 0], at(dzl=1))
            HF[n, 2 * y + zl] = total(zl)

    def stage_c(n):
        b = base(n)
        if ZSUM[n]:
            for d in (1, 3, 2):
                arrived(HR.at[n, 3 + d], xr.at[n, d])
            t = HF[n, 4 * zl + y]
            for d in (1, 2, 3):
                t = t + HR[n, 3 + d].astype(F32)
        else:
            arrived(HZR.at[n], xr.at[n, 0])
            t = HF[n, 2 * y + zl] + HZR[n]
        HG[b + zl, y] = t.astype(BF)
        own = HG.at[b + zl, y]
        send(own, own, xs.at[n, 8], xr.at[n, 8], at(dzl=1))
        for d in (1, 3, 2):
            send(own, own, xs.at[n, 8 + d], xr.at[n, 8 + d], at(dy=d))

    def stage_d(n):
        b = base(n)
        if ZGATHER[n]:
            theirs = HG.at[b + 1 - zl, y]
            arrived(theirs, xr.at[n, 8])
            for d in (1, 3, 2):
                send(theirs, theirs, xs.at[n, 11 + d], xr.at[n, 11 + d], at(dy=d))
        else:
            for d in (1, 3, 2):
                theirs = HG.at[b + zl, (y + 4 - d) % 4]
                arrived(theirs, xr.at[n, 8 + d])
                send(theirs, theirs, xs.at[n, 11 + d], xr.at[n, 11 + d], at(dzl=1))

    def stage_e(n):
        b = base(n)
        for d in (1, 3, 2):
            yy = (y + 4 - d) % 4
            if ZGATHER[n]:
                arrived(HG.at[b + zl, yy], xr.at[n, 8 + d])
            arrived(HG.at[b + 1 - zl, yy], xr.at[n, 11 + d])
        if not ZGATHER[n]:
            arrived(HG.at[b + 1 - zl, y], xr.at[n, 8])
        def tile(t, _):
            i, j = b + t // 8, t % 8
            rows = pl.ds(pl.multiple_of(j * 16, 16), 16)
            hg = HG[i, j // 2, pl.ds(pl.multiple_of((j % 2) * 16, 16), 16), :].astype(F32)
            DU[k, i, rows, :] = (hg * FU[i, rows, :]).astype(BF)
            DG[k, i, rows, :] = (hg * FG[i, rows, :]).astype(BF)
            return 0

        lax.fori_loop(0, 16, tile, 0)
        for j, buf in enumerate((DG, DU)):
            part = buf.at[k, pl.ds(b, 2)]
            send(part, part, ss.at[5 + 3 * n + j], sr.at[5 + 3 * n + j], at(dk=1))

    def stage_p(n):
        b = base(n)

        def tile(t, _):
            i, j = b + t // 8, t % 8
            rows = pl.ds(pl.multiple_of(j * 16, 16), 16)
            ga = GA[i, rows, :].astype(F32)
            up = UP[i, rows, :].astype(F32)
            sig = jax.nn.sigmoid(ga)
            gs = ga * sig
            HID[k, i, rows, :] = (gs * up).astype(BF)
            FU[i, rows, :] = gs
            FG[i, rows, :] = up * sig * (1.0 + ga * (1.0 - sig))
            return 0

        lax.fori_loop(0, 16, tile, 0)
        part = HID.at[k, pl.ds(b, 2)]
        send(part, part, ss.at[7 + 3 * n], sr.at[7 + 3 * n], at(dk=1))

    def stage_f(n):
        b = base(n)
        if n == 0:
            loads[5].wait()
            loads[6].wait()
        for j, buf in enumerate((DG, DU)):
            arrived(buf.at[1 - k, pl.ds(b, 2)], sr.at[5 + 3 * n + j])
        for q in (1, 0):
            p = (zh + q) % 2
            part = dot_nt(DG[p, pl.ds(b, 2)].reshape(2 * T, F), WG[...])
            part = part + dot_nt(DU[p, pl.ds(b, 2)].reshape(2 * T, F), WU[...])
            part = part.reshape(2, T, D)
            if n == 2:
                IPS[n, q] = part.astype(BF)
                for e in (1, 3) if q else (2,):
                    send(IPS.at[n, q, (zh + e) % 4 // 2], IZ2.at[e - 1], rs.at[2, 4 + e], rr.at[2, 4 + e], at(dzh=e))
                if q == 0:
                    IPO[2] = part
            elif order[n]:
                IPS[n, q] = part.astype(BF)
                send(IPS.at[n, q], IPR.at[n, q], xs.at[n, 15 + q], xr.at[n, 15 + q], at(dx=4 - order[n]))
            else:
                IPO[q] = part

    def sum_z2():
        t = IPO[2, zh // 2]
        for e in (1, 3, 2):
            arrived(IZ2.at[e - 1], rr.at[2, 4 + e])
            t = t + IZ2[e - 1].astype(F32)
        IXS[...] = t.astype(BF)
        send(IXS, IXR, rs.at[2, 8], rr.at[2, 8], at(dx=2))

    def sum_x(q):
        for n in range(2):
            arrived(IPR.at[n, q], xr.at[n, 15 + q])
        for i in range(2):
            t = IPO[q, i]
            for n in range(2):
                t = t + IPR[n, q, i].astype(F32)
            IZS[q, i] = t.astype(BF)
            IPO[q, i] = t
        for e in (1, 3) if q else (2,):
            send(IZS.at[q, (zh + e) % 4 // 2], IZR.at[e - 1], rs.at[2, e], rr.at[2, e], at(dzh=e))

    def send_zl():
        for i, src, buf in ((0, gate_in, GA), (1, up_in, UP)):
            send(src, buf.at[mine], rs.at[i, 0], rr.at[i, 0], at(dzl=1))

    def input_z():
        for e in (1, 3):
            send(x_in, XF.at[myp, myh], bs.at[1, e, 0], br.at[1, e, 0], at(dzh=e))

    def input_x():
        for d in (1, 3):
            send(x_in, XF.at[myp, myh], bs.at[1, 0, d], br.at[1, 0, d], at(dx=d))

    def gates_here():
        loads[2].wait()
        loads[3].wait()
        for i, buf in ((0, GA), (1, UP)):
            wait_y(i, buf, zl, 0)
            wait_y(i, buf, 1 - zl, 5)

    outs = []

    def weight_grad(i, lhs, rhs, out):
        if i == 0:
            for n in range(4):
                arrived(HID.at[1 - k, pl.ds(base(n), 2)], sr.at[7 + 3 * n])
        if i == 1:
            loads[4].wait()
            wait_x(XF, 1, 2)
        OUT[i] = dot_tn(lhs[...].reshape(16 * T, D), rhs[...].reshape(16 * T, F))
        cp = pltpu.make_async_copy(OUT.at[i], out, osem.at[i])
        cp.start()
        outs.append(cp)

    forward_x(GF, 0, 0)
    forward_z(GF, 0, 1)
    forward_z(GF, 0, 3)
    input_x()
    forward_y(0, GA, zl, 0)
    forward_y(1, UP, zl, 0)
    forward_z(GF, 0, 2)
    send_zl()
    to_sibling(3)
    forward_x(GF, 0, 1)
    forward_x(GF, 0, 3)
    stage_a(3)
    input_z()
    forward_x(GF, 0, 2)
    to_sibling(0)
    to_sibling(1)
    stage_a(0)
    stage_a(1)
    forward_zl(0, GA)
    forward_zl(1, UP)
    to_sibling(2)
    stage_a(2)
    stage_b(0)
    forward_x(XF, 1, 0)
    forward_z(XF, 1, 1)
    forward_z(XF, 1, 3)
    stage_b(3)
    stage_b(1)
    stage_c(0)
    forward_z(XF, 1, 2)
    stage_b(2)
    stage_c(1)
    forward_y(0, GA, 1 - zl, 5)
    forward_y(1, UP, 1 - zl, 5)
    stage_d(0)
    stage_c(2)
    forward_x(XF, 1, 1)
    forward_x(XF, 1, 3)
    forward_x(XF, 1, 2)
    stage_d(1)
    stage_c(3)
    stage_d(2)
    gates_here()
    stage_p(0)
    stage_e(0)
    stage_p(1)
    stage_p(2)
    stage_f(0)
    stage_e(1)
    stage_d(3)
    stage_p(3)
    stage_f(1)
    stage_e(2)
    weight_grad(0, GF, HID, gd_out)
    stage_f(2)
    stage_e(3)
    stage_f(3)
    sum_z2()
    sum_x(1)
    sum_x(0)
    weight_grad(1, XF, DG, gg_out)
    weight_grad(2, XF, DU, gu_out)

    t = IPO[0, zh // 2]
    for e in (1, 2, 3):
        arrived(IZR.at[e - 1], rr.at[2, e])
        t = t + IZR[e - 1].astype(F32)
    arrived(IXR, rr.at[2, 8])
    t = t + IXR[...].astype(F32)
    IGO[...] = t.astype(BF)
    cp = pltpu.make_async_copy(IGO, ig_out, osem.at[3])
    cp.start()
    outs.append(cp)
    for cp in outs:
        cp.wait()
    for cp in started:
        cp.wait_send()


def grads(*args):
    any_spec = pl.BlockSpec(memory_space=pl.ANY)
    dma = pltpu.SemaphoreType.DMA
    return pl.pallas_call(
        kernel,
        out_shape=[
            jax.ShapeDtypeStruct((T, D), BF),
            jax.ShapeDtypeStruct((D, F), F32),
            jax.ShapeDtypeStruct((D, F), F32),
            jax.ShapeDtypeStruct((D, F), F32),
        ],
        in_specs=[any_spec] * 7,
        out_specs=[any_spec] * 4,
        scratch_shapes=[
            pltpu.VMEM((2, 8, T, D), BF),
            pltpu.VMEM((8, T, D), BF),
            pltpu.VMEM((2, 8, T, D), BF),
            pltpu.VMEM((8, T, F), BF),
            pltpu.VMEM((8, T, F), BF),
            pltpu.VMEM((8, T, F), F32),
            pltpu.VMEM((8, T, F), F32),
            pltpu.VMEM((4, 8, Q, F), BF),
            pltpu.VMEM((4, 8, Q, F), F32),
            pltpu.VMEM((4, 7, Q, F), BF),
            pltpu.VMEM((4, Q, F), F32),
            pltpu.VMEM((4, Q, F), F32),
            pltpu.VMEM((8, 4, Q, F), BF),
            pltpu.VMEM((2, 8, T, F), BF),
            pltpu.VMEM((2, 8, T, F), BF),
            pltpu.VMEM((2, 8, T, F), BF),
            pltpu.VMEM((3, 2, T, D), F32),
            pltpu.VMEM((3, 2, 2, T, D), BF),
            pltpu.VMEM((2, 2, 2, T, D), BF),
            pltpu.VMEM((3, T, D), BF),
            pltpu.VMEM((T, D), BF),
            pltpu.VMEM((T, D), BF),
            pltpu.VMEM((2, 2, T, D), BF),
            pltpu.VMEM((3, T, D), BF),
            pltpu.VMEM((D, F), BF),
            pltpu.VMEM((D, F), BF),
            pltpu.VMEM((D, F), BF),
            pltpu.VMEM((D, F), BF),
            pltpu.VMEM((3, D, F), F32),
            pltpu.VMEM((T, D), BF),
            dma((7,)),
            dma((4,)),
            dma((2, 4, 6)),
            dma((2, 4, 6)),
            dma((4, 17)),
            dma((4, 17)),
            dma((3, 10)),
            dma((3, 10)),
            dma((17,)),
            dma((17,)),
        ],
        compiler_params=pltpu.CompilerParams(
            collective_id=0, has_side_effects=True, vmem_limit_bytes=60 * 1024 * 1024
        ),
        cost_estimate=pl.CostEstimate(flops=12 * 2048 * D * F, bytes_accessed=10 << 20, transcendentals=0),
        name="swiglu_backward",
    )(*args)


def hand_over(*refs):
    for src, dst in zip(refs[:4], refs[4:]):
        dst[...] = src[...]


def body(*args):
    outs = grads(*args)
    specs = [pl.BlockSpec((o.shape[0] // 4, o.shape[1]), lambda i: (i, 0)) for o in outs]
    return pl.pallas_call(
        hand_over,
        grid=(4,),
        out_shape=[jax.ShapeDtypeStruct(o.shape, o.dtype) for o in outs],
        in_specs=specs,
        out_specs=specs,
        name="hand_over",
    )(*outs)


def solution(mesh):
    return jax.shard_map(
        body,
        mesh=mesh,
        in_specs=(
            P("col", "row"),
            P("col", "row"),
            P("row", "col"),
            P("row", "col"),
            P("row", "col"),
            P("row", "col"),
            P("row", "col"),
        ),
        out_specs=(P("col", "row"), P("row", "col"), P("row", "col"), P("row", "col")),
        check_vma=False,
    )
```

```python
import jax
import jax.numpy as jnp
from jax import lax
from jax.experimental import pallas as pl
from jax.experimental.pallas import tpu as pltpu
from jax.sharding import PartitionSpec as P

MESH = pl.DeviceIdType.MESH
BF = jnp.bfloat16
F32 = jnp.float32
T, D, F = 128, 512, 896
Q = 32
ZSUM = (0, 1, 1, 0)
ZGATHER = (1, 0, 1, 0)


def dot(a, b):
    return jnp.dot(a, b, preferred_element_type=F32)


def dot_nt(a, b):
    return lax.dot_general(a, b, (((1,), (1,)), ((), ())), preferred_element_type=F32)


def dot_tn(a, b):
    return lax.dot_general(a, b, (((0,), (0,)), ((), ())), preferred_element_type=F32)


def kernel(
    x_in, g_in, gate_in, up_in, wg_in, wu_in, wd_in,
    ig_out, gg_out, gu_out, gd_out,
    GF, GS, XF, GA, UP, FU, FG, HP, HF, HR, HZS, HZR, HG, HID, DG, DU,
    IPO, IPS, IPR, IZ2, IXS, IXR, IZS, IZR, WD, WDS, WG, WU, OUT, IGO,
    lsem, osem, bs, br, xs, xr, rs, rr, ss, sr,
):
    row = lax.axis_index("row")
    col = lax.axis_index("col")
    zl, y, k = row // 8, (row // 2) % 4, row % 2
    x, zh = col // 4, col % 4

    def at(dzl=0, dy=0, dk=0, dx=0, dzh=0):
        r = ((zl + dzl) % 2) * 8 + ((y + dy) % 4) * 2 + (k + dk) % 2
        c = ((x + dx) % 4) * 4 + (zh + dzh) % 4
        return {"row": r, "col": c}

    started = []

    def send(src, dst, send_sem, recv_sem, dev):
        cp = pltpu.make_async_remote_copy(
            src_ref=src, dst_ref=dst, send_sem=send_sem, recv_sem=recv_sem, device_id=dev, device_id_type=MESH
        )
        cp.start()
        started.append(cp)

    def arrived(dst, recv_sem):
        pltpu.make_async_copy(dst, dst, recv_sem).wait()

    def blk(xx, zz):
        xx, zz = (xx + 8) % 4, (zz + 8) % 4
        return zz % 2, 2 * xx + zz // 2

    myp, myh = blk(x, zh)
    mine = 4 * zl + y
    other = 4 * (1 - zl) + y

    loads = []
    for i, (src, dst) in enumerate(
        [
            (g_in, GF.at[myp, myh]), (wd_in, WD), (gate_in, GA.at[mine]), (up_in, UP.at[mine]),
            (x_in, XF.at[myp, myh]), (wg_in, WG), (wu_in, WU),
        ]
    ):
        cp = pltpu.make_async_copy(src, dst, lsem.at[i])
        cp.start()
        loads.append(cp)

    peers = [at(dk=1), at(dzl=1)]
    for d in (1, 2, 3):
        peers += [at(dy=d), at(dx=d), at(dzh=d)]
    barrier = pltpu.get_barrier_semaphore()
    for p in peers:
        pl.semaphore_signal(barrier, inc=1, device_id=p, device_id_type=MESH)
    pl.semaphore_wait(barrier, len(peers))

    for e in (1, 3):
        send(g_in, GF.at[myp, myh], bs.at[0, e, 0], br.at[0, e, 0], at(dzh=e))
    for d in (1, 3):
        send(g_in, GF.at[myp, myh], bs.at[0, 0, d], br.at[0, 0, d], at(dx=d))
    for i, src, buf in ((0, gate_in, GA), (1, up_in, UP)):
        for d in (1, 3):
            send(src, buf.at[mine], rs.at[i, d], rr.at[i, d], at(dy=d))
    send(wd_in, WDS, ss.at[0], sr.at[0], at(dk=1))

    HALF = (pl.ds(0, T // 2), pl.ds(T // 2, T // 2))

    def forward_z(buf, i, e):
        p, h = blk(x, zh - e)
        if e == 2:
            for j in range(2):
                arrived(buf.at[p, h, HALF[j]], br.at[i, 2, 5 * j])
        else:
            arrived(buf.at[p, h], br.at[i, e, 0])
            half = buf.at[p, h, HALF[e // 2]]
            send(half, half, bs.at[i, 2, 5 * (e // 2)], br.at[i, 2, 5 * (e // 2)], at(dzh=e))
        for d in (1, 3):
            send(buf.at[p, h], buf.at[p, h], bs.at[i, e, d], br.at[i, e, d], at(dx=d))

    def forward_x(buf, i, e):
        for j, d in enumerate((1, 3)):
            p, h = blk(x - d, zh - e)
            arrived(buf.at[p, h], br.at[i, e, d])
            half = buf.at[p, h, HALF[j]]
            send(half, half, bs.at[i, e, 2 + 2 * j], br.at[i, e, 2 + 2 * j], at(dx=d))

    def wait_x(buf, i, d):
        if d == 2:
            for e in range(4):
                p, h = blk(x - 2, zh - e)
                for j in range(2):
                    arrived(buf.at[p, h, HALF[j]], br.at[i, e, 2 + 2 * j])

    def forward_y(i, buf, z, o):
        for j, d in enumerate((1, 3)):
            h = 4 * z + (y + 4 - d) % 4
            arrived(buf.at[h], rr.at[i, o + d])
            half = buf.at[h, HALF[j]]
            send(half, half, rs.at[i, o + 2 + 2 * j], rr.at[i, o + 2 + 2 * j], at(dy=d))

    def wait_y(i, buf, z, o):
        for j in range(2):
            arrived(buf.at[4 * z + (y + 2) % 4, HALF[j]], rr.at[i, o + 2 + 2 * j])

    def forward_zl(i, buf):
        arrived(buf.at[other], rr.at[i, 0])
        for d in (1, 3):
            send(buf.at[other], buf.at[other], rs.at[i, 5 + d], rr.at[i, 5 + d], at(dy=d))

    order = (1, 3, 2, 0)

    def base(n):
        return 2 * ((x + 4 - order[n]) % 4)

    def to_sibling(n):
        if order[n]:
            wait_x(GF, 0, order[n])
        else:
            loads[0].wait()
        b = base(n)
        send(GF.at[1 - k, pl.ds(b, 2)], GS.at[pl.ds(b, 2)], ss.at[1 + n], sr.at[1 + n], at(dk=1))

    def stage_a(n):
        b = base(n)
        arrived(GS.at[pl.ds(b, 2)], sr.at[1 + n])
        if n == 3:
            loads[1].wait()
            arrived(WDS, sr.at[0])
        part = dot(GF[k, pl.ds(b, 2)].reshape(2 * T, D), WD[...])
        part = (part + dot(GS[pl.ds(b, 2)].reshape(2 * T, D), WDS[...])).reshape(2, 4, Q, F)
        if ZSUM[n]:
            part = part.reshape(8, Q, F)
            HF[n] = part
            HP[n] = part.astype(BF)
            if ZSUM[n] == 2:
                for j in (4, 1, 3, 5, 7, 2, 6):
                    to = (zl + j // 4) % 2 * 4 + (y + j) % 4
                    send(HP.at[n, to], HR.at[n, j - 1], xs.at[n, j], xr.at[n, j], at(dzl=j // 4, dy=j % 4))
            else:
                send(HP.at[n, pl.ds(4 * (1 - zl), 4)], HR.at[n, pl.ds(0, 4)], xs.at[n, 0], xr.at[n, 0], at(dzl=1))
        else:
            for yy in range(4):
                HF[n, 2 * yy : 2 * yy + 2] = part[:, yy]
                HP[n, 2 * yy : 2 * yy + 2] = part[:, yy].astype(BF)
            for d in (1, 3, 2):
                to = 2 * ((y + d) % 4)
                send(HP.at[n, pl.ds(to, 2)], HR.at[n, pl.ds(2 * d - 2, 2)], xs.at[n, d], xr.at[n, d], at(dy=d))

    def stage_b(n):
        if ZSUM[n] == 2:
            return
        if ZSUM[n]:
            arrived(HR.at[n, pl.ds(0, 4)], xr.at[n, 0])
            for yy in range(4):
                t = HF[n, 4 * zl + yy] + HR[n, yy].astype(F32)
                HF[n, 4 * zl + yy] = t
                HP[n, 4 * zl + yy] = t.astype(BF)
            for d in (1, 3, 2):
                to = 4 * zl + (y + d) % 4
                send(HP.at[n, to], HR.at[n, 3 + d], xs.at[n, d], xr.at[n, d], at(dy=d))
        else:
            for d in (1, 3, 2):
                arrived(HR.at[n, pl.ds(2 * d - 2, 2)], xr.at[n, d])

            def total(z):
                t = HF[n, 2 * y + z]
                for d in (1, 2, 3):
                    t = t + HR[n, 2 * d - 2 + z].astype(F32)
                return t

            HZS[n] = total(1 - zl).astype(BF)
            send(HZS.at[n], HZR.at[n], xs.at[n, 0], xr.at[n, 0], at(dzl=1))
            HF[n, 2 * y + zl] = total(zl)

    def stage_c(n):
        b = base(n)
        if ZSUM[n] == 2:
            t = HF[n, 4 * zl + y]
            for j in (4, 1, 3, 5, 7, 2, 6):
                arrived(HR.at[n, j - 1], xr.at[n, j])
                t = t + HR[n, j - 1].astype(F32)
        elif ZSUM[n]:
            for d in (1, 3, 2):
                arrived(HR.at[n, 3 + d], xr.at[n, d])
            t = HF[n, 4 * zl + y]
            for d in (1, 2, 3):
                t = t + HR[n, 3 + d].astype(F32)
        else:
            arrived(HZR.at[n], xr.at[n, 0])
            t = HF[n, 2 * y + zl] + HZR[n].astype(F32)
        HG[b + zl, y] = t.astype(BF)
        own = HG.at[b + zl, y]
        send(own, own, xs.at[n, 8], xr.at[n, 8], at(dzl=1))
        for d in (1, 3, 2):
            send(own, own, xs.at[n, 8 + d], xr.at[n, 8 + d], at(dy=d))
        if ZGATHER[n] == 2:
            for d in (1, 3, 2):
                send(own, own, xs.at[n, 11 + d], xr.at[n, 11 + d], at(dzl=1, dy=d))

    def stage_d(n):
        b = base(n)
        if ZGATHER[n] == 2:
            return
        if ZGATHER[n]:
            theirs = HG.at[b + 1 - zl, y]
            arrived(theirs, xr.at[n, 8])
            for d in (1, 3, 2):
                send(theirs, theirs, xs.at[n, 11 + d], xr.at[n, 11 + d], at(dy=d))
        else:
            for d in (1, 3, 2):
                theirs = HG.at[b + zl, (y + 4 - d) % 4]
                arrived(theirs, xr.at[n, 8 + d])
                send(theirs, theirs, xs.at[n, 11 + d], xr.at[n, 11 + d], at(dzl=1))

    def stage_e(n):
        b = base(n)
        for d in (1, 3, 2):
            yy = (y + 4 - d) % 4
            if ZGATHER[n]:
                arrived(HG.at[b + zl, yy], xr.at[n, 8 + d])
            arrived(HG.at[b + 1 - zl, yy], xr.at[n, 11 + d])
        if ZGATHER[n] != 1:
            arrived(HG.at[b + 1 - zl, y], xr.at[n, 8])
        def tile(t, _):
            i, j = b + t // 8, t % 8
            rows = pl.ds(pl.multiple_of(j * 16, 16), 16)
            hg = HG[i, j // 2, pl.ds(pl.multiple_of((j % 2) * 16, 16), 16), :].astype(F32)
            DU[k, i, rows, :] = (hg * FU[i, rows, :]).astype(BF)
            DG[k, i, rows, :] = (hg * FG[i, rows, :]).astype(BF)
            return 0

        lax.fori_loop(0, 16, tile, 0)
        for j, buf in enumerate((DG, DU)):
            part = buf.at[k, pl.ds(b, 2)]
            send(part, part, ss.at[5 + 3 * n + j], sr.at[5 + 3 * n + j], at(dk=1))

    def stage_p(n):
        b = base(n)

        def tile(t, _):
            i, j = b + t // 8, t % 8
            rows = pl.ds(pl.multiple_of(j * 16, 16), 16)
            ga = GA[i, rows, :].astype(F32)
            up = UP[i, rows, :].astype(F32)
            sig = jax.nn.sigmoid(ga)
            gs = ga * sig
            HID[k, i, rows, :] = (gs * up).astype(BF)
            FU[i, rows, :] = gs
            FG[i, rows, :] = up * sig * (1.0 + ga * (1.0 - sig))
            return 0

        lax.fori_loop(0, 16, tile, 0)
        part = HID.at[k, pl.ds(b, 2)]
        send(part, part, ss.at[7 + 3 * n], sr.at[7 + 3 * n], at(dk=1))

    def stage_f(n):
        b = base(n)
        if n == 0:
            loads[5].wait()
            loads[6].wait()
        for j, buf in enumerate((DG, DU)):
            arrived(buf.at[1 - k, pl.ds(b, 2)], sr.at[5 + 3 * n + j])
        for q in (1, 0):
            p = (zh + q) % 2
            part = dot_nt(DG[p, pl.ds(b, 2)].reshape(2 * T, F), WG[...])
            part = part + dot_nt(DU[p, pl.ds(b, 2)].reshape(2 * T, F), WU[...])
            part = part.reshape(2, T, D)
            if n == 2:
                IPS[n, q] = part.astype(BF)
                for e in (1, 3) if q else (2,):
                    send(IPS.at[n, q, (zh + e) % 4 // 2], IZ2.at[e - 1], rs.at[2, 4 + e], rr.at[2, 4 + e], at(dzh=e))
                if q == 0:
                    IPO[2] = part
            elif order[n]:
                IPS[n, q] = part.astype(BF)
                send(IPS.at[n, q], IPR.at[n, q], xs.at[n, 15 + q], xr.at[n, 15 + q], at(dx=4 - order[n]))
            else:
                IPO[q] = part

    def sum_z2():
        t = IPO[2, zh // 2]
        for e in (1, 3, 2):
            arrived(IZ2.at[e - 1], rr.at[2, 4 + e])
            t = t + IZ2[e - 1].astype(F32)
        IXS[...] = t.astype(BF)
        send(IXS, IXR, rs.at[2, 8], rr.at[2, 8], at(dx=2))

    def sum_x(q):
        for n in range(2):
            arrived(IPR.at[n, q], xr.at[n, 15 + q])
        for i in range(2):
            t = IPO[q, i]
            for n in range(2):
                t = t + IPR[n, q, i].astype(F32)
            IZS[q, i] = t.astype(BF)
            IPO[q, i] = t
        for e in (1, 3) if q else (2,):
            send(IZS.at[q, (zh + e) % 4 // 2], IZR.at[e - 1], rs.at[2, e], rr.at[2, e], at(dzh=e))

    def send_zl():
        for i, src, buf in ((0, gate_in, GA), (1, up_in, UP)):
            send(src, buf.at[mine], rs.at[i, 0], rr.at[i, 0], at(dzl=1))

    def input_z():
        for e in (1, 3):
            send(x_in, XF.at[myp, myh], bs.at[1, e, 0], br.at[1, e, 0], at(dzh=e))

    def input_x():
        for d in (1, 3):
            send(x_in, XF.at[myp, myh], bs.at[1, 0, d], br.at[1, 0, d], at(dx=d))

    def gates_here():
        loads[2].wait()
        loads[3].wait()
        for i, buf in ((0, GA), (1, UP)):
            wait_y(i, buf, zl, 0)
            wait_y(i, buf, 1 - zl, 5)

    outs = []

    def weight_grad(i, lhs, rhs, out):
        if i == 0:
            for n in range(4):
                arrived(HID.at[1 - k, pl.ds(base(n), 2)], sr.at[7 + 3 * n])
        if i == 1:
            loads[4].wait()
            wait_x(XF, 1, 2)
        OUT[i] = dot_tn(lhs[...].reshape(16 * T, D), rhs[...].reshape(16 * T, F))
        cp = pltpu.make_async_copy(OUT.at[i], out, osem.at[i])
        cp.start()
        outs.append(cp)

    forward_x(GF, 0, 0)
    forward_z(GF, 0, 1)
    forward_z(GF, 0, 3)
    forward_y(0, GA, zl, 0)
    forward_y(1, UP, zl, 0)
    forward_z(GF, 0, 2)
    send_zl()
    to_sibling(3)
    forward_x(GF, 0, 1)
    forward_x(GF, 0, 3)
    stage_a(3)
    input_x()
    input_z()
    forward_x(GF, 0, 2)
    to_sibling(0)
    to_sibling(1)
    stage_a(0)
    stage_a(1)
    forward_zl(0, GA)
    forward_zl(1, UP)
    to_sibling(2)
    stage_a(2)
    stage_b(0)
    forward_x(XF, 1, 0)
    stage_b(1)
    stage_c(0)
    forward_z(XF, 1, 1)
    forward_z(XF, 1, 3)
    stage_b(2)
    forward_y(0, GA, 1 - zl, 5)
    forward_y(1, UP, 1 - zl, 5)
    stage_c(1)
    stage_d(0)
    forward_z(XF, 1, 2)
    stage_c(2)
    stage_d(1)
    stage_b(3)
    gates_here()
    stage_p(0)
    stage_e(0)
    stage_p(1)
    stage_d(2)
    stage_f(0)
    forward_x(XF, 1, 1)
    forward_x(XF, 1, 3)
    stage_c(3)
    stage_e(1)
    stage_p(2)
    stage_f(1)
    forward_x(XF, 1, 2)
    stage_e(2)
    stage_d(3)
    stage_f(2)
    stage_p(3)
    stage_e(3)
    stage_f(3)
    sum_z2()
    sum_x(1)
    sum_x(0)
    weight_grad(0, GF, HID, gd_out)
    weight_grad(1, XF, DG, gg_out)
    weight_grad(2, XF, DU, gu_out)

    t = IPO[0, zh // 2]
    for e in (1, 2, 3):
        arrived(IZR.at[e - 1], rr.at[2, e])
        t = t + IZR[e - 1].astype(F32)
    arrived(IXR, rr.at[2, 8])
    t = t + IXR[...].astype(F32)
    IGO[...] = t.astype(BF)
    cp = pltpu.make_async_copy(IGO, ig_out, osem.at[3])
    cp.start()
    outs.append(cp)
    for cp in outs:
        cp.wait()
    for cp in started:
        cp.wait_send()


def grads(*args):
    any_spec = pl.BlockSpec(memory_space=pl.ANY)
    dma = pltpu.SemaphoreType.DMA
    return pl.pallas_call(
        kernel,
        out_shape=[
            jax.ShapeDtypeStruct((T, D), BF),
            jax.ShapeDtypeStruct((D, F), F32),
            jax.ShapeDtypeStruct((D, F), F32),
            jax.ShapeDtypeStruct((D, F), F32),
        ],
        in_specs=[any_spec] * 7,
        out_specs=[any_spec] * 4,
        scratch_shapes=[
            pltpu.VMEM((2, 8, T, D), BF),
            pltpu.VMEM((8, T, D), BF),
            pltpu.VMEM((2, 8, T, D), BF),
            pltpu.VMEM((8, T, F), BF),
            pltpu.VMEM((8, T, F), BF),
            pltpu.VMEM((8, T, F), F32),
            pltpu.VMEM((8, T, F), F32),
            pltpu.VMEM((4, 8, Q, F), BF),
            pltpu.VMEM((4, 8, Q, F), F32),
            pltpu.VMEM((4, 7, Q, F), BF),
            pltpu.VMEM((4, Q, F), BF),
            pltpu.VMEM((4, Q, F), BF),
            pltpu.VMEM((8, 4, Q, F), BF),
            pltpu.VMEM((2, 8, T, F), BF),
            pltpu.VMEM((2, 8, T, F), BF),
            pltpu.VMEM((2, 8, T, F), BF),
            pltpu.VMEM((3, 2, T, D), F32),
            pltpu.VMEM((3, 2, 2, T, D), BF),
            pltpu.VMEM((2, 2, 2, T, D), BF),
            pltpu.VMEM((3, T, D), BF),
            pltpu.VMEM((T, D), BF),
            pltpu.VMEM((T, D), BF),
            pltpu.VMEM((2, 2, T, D), BF),
            pltpu.VMEM((3, T, D), BF),
            pltpu.VMEM((D, F), BF),
            pltpu.VMEM((D, F), BF),
            pltpu.VMEM((D, F), BF),
            pltpu.VMEM((D, F), BF),
            pltpu.VMEM((3, D, F), F32),
            pltpu.VMEM((T, D), BF),
            dma((7,)),
            dma((4,)),
            dma((2, 4, 6)),
            dma((2, 4, 6)),
            dma((4, 17)),
            dma((4, 17)),
            dma((3, 10)),
            dma((3, 10)),
            dma((17,)),
            dma((17,)),
        ],
        compiler_params=pltpu.CompilerParams(
            collective_id=0, has_side_effects=True, vmem_limit_bytes=60 * 1024 * 1024
        ),
        cost_estimate=pl.CostEstimate(flops=12 * 2048 * D * F, bytes_accessed=10 << 20, transcendentals=0),
        name="swiglu_backward",
    )(*args)


def hand_over(*refs):
    for src, dst in zip(refs[:4], refs[4:]):
        dst[...] = src[...]


def body(*args):
    outs = grads(*args)
    specs = [pl.BlockSpec((o.shape[0] // 2, o.shape[1]), lambda i: (i, 0)) for o in outs]
    return pl.pallas_call(
        hand_over,
        grid=(2,),
        out_shape=[jax.ShapeDtypeStruct(o.shape, o.dtype) for o in outs],
        in_specs=specs,
        out_specs=specs,
        name="hand_over",
    )(*outs)


def solution(mesh):
    return jax.shard_map(
        body,
        mesh=mesh,
        in_specs=(
            P("col", "row"),
            P("col", "row"),
            P("row", "col"),
            P("row", "col"),
            P("row", "col"),
            P("row", "col"),
            P("row", "col"),
        ),
        out_specs=(P("col", "row"), P("row", "col"), P("row", "col"), P("row", "col")),
        check_vma=False,
    )
```

```python
import jax
import jax.numpy as jnp
from jax import lax
from jax.experimental import pallas as pl
from jax.experimental.pallas import tpu as pltpu
from jax.sharding import PartitionSpec as P

MESH = pl.DeviceIdType.MESH
BF = jnp.bfloat16
F32 = jnp.float32
T, D, F = 128, 512, 896
Q = 32
ZSUM = (0, 1, 1, 0)
ZGATHER = (1, 0, 1, 0)


def dot(a, b):
    return jnp.dot(a, b, preferred_element_type=F32)


def dot_nt(a, b):
    return lax.dot_general(a, b, (((1,), (1,)), ((), ())), preferred_element_type=F32)


def dot_tn(a, b):
    return lax.dot_general(a, b, (((0,), (0,)), ((), ())), preferred_element_type=F32)


def kernel(
    x_in, g_in, gate_in, up_in, wg_in, wu_in, wd_in,
    ig_out, gg_out, gu_out, gd_out,
    GF, GS, XF, GA, UP, FU, FG, HP, HF, HR, HZS, HZR, HG, HID, DG, DU,
    IPO, IPS, IPR, IZ2, IXS, IXR, IZS, IZR, WD, WDS, WG, WU, OUT, IGO,
    lsem, osem, bs, br, xs, xr, rs, rr, ss, sr,
):
    row = lax.axis_index("row")
    col = lax.axis_index("col")
    zl, y, k = row // 8, (row // 2) % 4, row % 2
    x, zh = col // 4, col % 4

    def at(dzl=0, dy=0, dk=0, dx=0, dzh=0):
        r = ((zl + dzl) % 2) * 8 + ((y + dy) % 4) * 2 + (k + dk) % 2
        c = ((x + dx) % 4) * 4 + (zh + dzh) % 4
        return {"row": r, "col": c}

    started = []

    def send(src, dst, send_sem, recv_sem, dev):
        cp = pltpu.make_async_remote_copy(
            src_ref=src, dst_ref=dst, send_sem=send_sem, recv_sem=recv_sem, device_id=dev, device_id_type=MESH
        )
        cp.start()
        started.append(cp)

    def arrived(dst, recv_sem):
        pltpu.make_async_copy(dst, dst, recv_sem).wait()

    def blk(xx, zz):
        xx, zz = (xx + 8) % 4, (zz + 8) % 4
        return zz % 2, 2 * xx + zz // 2

    myp, myh = blk(x, zh)
    mine = 4 * zl + y
    other = 4 * (1 - zl) + y

    loads = []
    for i, (src, dst) in enumerate(
        [
            (g_in, GF.at[myp, myh]), (wd_in, WD), (gate_in, GA.at[mine]), (up_in, UP.at[mine]),
            (x_in, XF.at[myp, myh]), (wg_in, WG), (wu_in, WU),
        ]
    ):
        cp = pltpu.make_async_copy(src, dst, lsem.at[i])
        cp.start()
        loads.append(cp)

    peers = [at(dk=1), at(dzl=1)]
    for d in (1, 2, 3):
        peers += [at(dy=d), at(dx=d), at(dzh=d)]
    barrier = pltpu.get_barrier_semaphore()
    for p in peers:
        pl.semaphore_signal(barrier, inc=1, device_id=p, device_id_type=MESH)
    pl.semaphore_wait(barrier, len(peers))

    for e in (1, 3):
        send(g_in, GF.at[myp, myh], bs.at[0, e, 0], br.at[0, e, 0], at(dzh=e))
    for d in (1, 3):
        send(g_in, GF.at[myp, myh], bs.at[0, 0, d], br.at[0, 0, d], at(dx=d))
    for i, src, buf in ((0, gate_in, GA), (1, up_in, UP)):
        for d in (1, 3):
            send(src, buf.at[mine], rs.at[i, d], rr.at[i, d], at(dy=d))
    send(wd_in, WDS, ss.at[0], sr.at[0], at(dk=1))

    HALF = (pl.ds(0, T // 2), pl.ds(T // 2, T // 2))

    def forward_z(buf, i, e):
        p, h = blk(x, zh - e)
        if e == 2:
            for j in range(2):
                arrived(buf.at[p, h, HALF[j]], br.at[i, 2, 5 * j])
        else:
            arrived(buf.at[p, h], br.at[i, e, 0])
            half = buf.at[p, h, HALF[e // 2]]
            send(half, half, bs.at[i, 2, 5 * (e // 2)], br.at[i, 2, 5 * (e // 2)], at(dzh=e))
        for d in (1, 3):
            send(buf.at[p, h], buf.at[p, h], bs.at[i, e, d], br.at[i, e, d], at(dx=d))

    def forward_x(buf, i, e):
        for j, d in enumerate((1, 3)):
            p, h = blk(x - d, zh - e)
            arrived(buf.at[p, h], br.at[i, e, d])
            half = buf.at[p, h, HALF[j]]
            send(half, half, bs.at[i, e, 2 + 2 * j], br.at[i, e, 2 + 2 * j], at(dx=d))

    def wait_x(buf, i, d):
        if d == 2:
            for e in range(4):
                p, h = blk(x - 2, zh - e)
                for j in range(2):
                    arrived(buf.at[p, h, HALF[j]], br.at[i, e, 2 + 2 * j])

    def forward_y(i, buf, z, o):
        for j, d in enumerate((1, 3)):
            h = 4 * z + (y + 4 - d) % 4
            arrived(buf.at[h], rr.at[i, o + d])
            half = buf.at[h, HALF[j]]
            send(half, half, rs.at[i, o + 2 + 2 * j], rr.at[i, o + 2 + 2 * j], at(dy=d))

    def wait_y(i, buf, z, o):
        for j in range(2):
            arrived(buf.at[4 * z + (y + 2) % 4, HALF[j]], rr.at[i, o + 2 + 2 * j])

    def forward_zl(i, buf):
        arrived(buf.at[other], rr.at[i, 0])
        for d in (1, 3):
            send(buf.at[other], buf.at[other], rs.at[i, 5 + d], rr.at[i, 5 + d], at(dy=d))

    order = (1, 3, 2, 0)

    def base(n):
        return 2 * ((x + 4 - order[n]) % 4)

    def to_sibling(n):
        if order[n]:
            wait_x(GF, 0, order[n])
        else:
            loads[0].wait()
        b = base(n)
        send(GF.at[1 - k, pl.ds(b, 2)], GS.at[pl.ds(b, 2)], ss.at[1 + n], sr.at[1 + n], at(dk=1))

    def stage_a(n):
        b = base(n)
        arrived(GS.at[pl.ds(b, 2)], sr.at[1 + n])
        if n == 3:
            loads[1].wait()
            arrived(WDS, sr.at[0])
        part = dot(GF[k, pl.ds(b, 2)].reshape(2 * T, D), WD[...])
        part = (part + dot(GS[pl.ds(b, 2)].reshape(2 * T, D), WDS[...])).reshape(2, 4, Q, F)
        if ZSUM[n]:
            part = part.reshape(8, Q, F)
            HF[n] = part
            HP[n] = part.astype(BF)
            if ZSUM[n] == 2:
                for j in (4, 1, 3, 5, 7, 2, 6):
                    to = (zl + j // 4) % 2 * 4 + (y + j) % 4
                    send(HP.at[n, to], HR.at[n, j - 1], xs.at[n, j], xr.at[n, j], at(dzl=j // 4, dy=j % 4))
            else:
                send(HP.at[n, pl.ds(4 * (1 - zl), 4)], HR.at[n, pl.ds(0, 4)], xs.at[n, 0], xr.at[n, 0], at(dzl=1))
        else:
            for yy in range(4):
                HF[n, 2 * yy : 2 * yy + 2] = part[:, yy]
                HP[n, 2 * yy : 2 * yy + 2] = part[:, yy].astype(BF)
            for d in (2, 1, 3):
                to = 2 * ((y + d) % 4)
                send(HP.at[n, pl.ds(to, 2)], HR.at[n, pl.ds(2 * d - 2, 2)], xs.at[n, d], xr.at[n, d], at(dy=d))

    def stage_b(n):
        if ZSUM[n] == 2:
            return
        if ZSUM[n]:
            arrived(HR.at[n, pl.ds(0, 4)], xr.at[n, 0])
            for yy in range(4):
                t = HF[n, 4 * zl + yy] + HR[n, yy].astype(F32)
                HF[n, 4 * zl + yy] = t
                HP[n, 4 * zl + yy] = t.astype(BF)
            for d in (2, 1, 3):
                to = 4 * zl + (y + d) % 4
                send(HP.at[n, to], HR.at[n, 3 + d], xs.at[n, d], xr.at[n, d], at(dy=d))
        else:
            for d in (2, 1, 3):
                arrived(HR.at[n, pl.ds(2 * d - 2, 2)], xr.at[n, d])

            def total(z):
                t = HF[n, 2 * y + z]
                for d in (1, 2, 3):
                    t = t + HR[n, 2 * d - 2 + z].astype(F32)
                return t

            HZS[n] = total(1 - zl).astype(BF)
            send(HZS.at[n], HZR.at[n], xs.at[n, 0], xr.at[n, 0], at(dzl=1))
            HF[n, 2 * y + zl] = total(zl)

    def stage_c(n):
        b = base(n)
        if ZSUM[n] == 2:
            t = HF[n, 4 * zl + y]
            for j in (4, 1, 3, 5, 7, 2, 6):
                arrived(HR.at[n, j - 1], xr.at[n, j])
                t = t + HR[n, j - 1].astype(F32)
        elif ZSUM[n]:
            for d in (2, 1, 3):
                arrived(HR.at[n, 3 + d], xr.at[n, d])
            t = HF[n, 4 * zl + y]
            for d in (1, 2, 3):
                t = t + HR[n, 3 + d].astype(F32)
        else:
            arrived(HZR.at[n], xr.at[n, 0])
            t = HF[n, 2 * y + zl] + HZR[n].astype(F32)
        HG[b + zl, y] = t.astype(BF)
        own = HG.at[b + zl, y]
        send(own, own, xs.at[n, 8], xr.at[n, 8], at(dzl=1))
        for d in (2, 1, 3):
            send(own, own, xs.at[n, 8 + d], xr.at[n, 8 + d], at(dy=d))
        if ZGATHER[n] == 2:
            for d in (2, 1, 3):
                send(own, own, xs.at[n, 11 + d], xr.at[n, 11 + d], at(dzl=1, dy=d))

    def stage_d(n):
        b = base(n)
        if ZGATHER[n] == 2:
            return
        if ZGATHER[n]:
            theirs = HG.at[b + 1 - zl, y]
            arrived(theirs, xr.at[n, 8])
            for d in (2, 1, 3):
                send(theirs, theirs, xs.at[n, 11 + d], xr.at[n, 11 + d], at(dy=d))
        else:
            for d in (2, 1, 3):
                theirs = HG.at[b + zl, (y + 4 - d) % 4]
                arrived(theirs, xr.at[n, 8 + d])
                send(theirs, theirs, xs.at[n, 11 + d], xr.at[n, 11 + d], at(dzl=1))

    def stage_e(n):
        b = base(n)
        for d in (2, 1, 3):
            yy = (y + 4 - d) % 4
            if ZGATHER[n]:
                arrived(HG.at[b + zl, yy], xr.at[n, 8 + d])
            arrived(HG.at[b + 1 - zl, yy], xr.at[n, 11 + d])
        if ZGATHER[n] != 1:
            arrived(HG.at[b + 1 - zl, y], xr.at[n, 8])
        def tile(t, _):
            i, j = b + t // 8, t % 8
            rows = pl.ds(pl.multiple_of(j * 16, 16), 16)
            hg = HG[i, j // 2, pl.ds(pl.multiple_of((j % 2) * 16, 16), 16), :].astype(F32)
            DU[k, i, rows, :] = (hg * FU[i, rows, :]).astype(BF)
            DG[k, i, rows, :] = (hg * FG[i, rows, :]).astype(BF)
            return 0

        lax.fori_loop(0, 16, tile, 0)
        for j, buf in enumerate((DG, DU)):
            part = buf.at[k, pl.ds(b, 2)]
            send(part, part, ss.at[5 + 3 * n + j], sr.at[5 + 3 * n + j], at(dk=1))

    def stage_p(n):
        b = base(n)

        def tile(t, _):
            i, j = b + t // 8, t % 8
            rows = pl.ds(pl.multiple_of(j * 16, 16), 16)
            ga = GA[i, rows, :].astype(F32)
            up = UP[i, rows, :].astype(F32)
            sig = jax.nn.sigmoid(ga)
            gs = ga * sig
            HID[k, i, rows, :] = (gs * up).astype(BF)
            FU[i, rows, :] = gs
            FG[i, rows, :] = up * sig * (1.0 + ga * (1.0 - sig))
            return 0

        lax.fori_loop(0, 16, tile, 0)
        part = HID.at[k, pl.ds(b, 2)]
        send(part, part, ss.at[7 + 3 * n], sr.at[7 + 3 * n], at(dk=1))

    def stage_f(n):
        b = base(n)
        if n == 0:
            loads[5].wait()
            loads[6].wait()
        for j, buf in enumerate((DG, DU)):
            arrived(buf.at[1 - k, pl.ds(b, 2)], sr.at[5 + 3 * n + j])
        for q in (1, 0):
            p = (zh + q) % 2
            part = dot_nt(DG[p, pl.ds(b, 2)].reshape(2 * T, F), WG[...])
            part = part + dot_nt(DU[p, pl.ds(b, 2)].reshape(2 * T, F), WU[...])
            part = part.reshape(2, T, D)
            if n == 2:
                IPS[n, q] = part.astype(BF)
                for e in (1, 3) if q else (2,):
                    send(IPS.at[n, q, (zh + e) % 4 // 2], IZ2.at[e - 1], rs.at[2, 4 + e], rr.at[2, 4 + e], at(dzh=e))
                if q == 0:
                    IPO[2] = part
            elif order[n]:
                IPS[n, q] = part.astype(BF)
                send(IPS.at[n, q], IPR.at[n, q], xs.at[n, 15 + q], xr.at[n, 15 + q], at(dx=4 - order[n]))
            else:
                IPO[q] = part

    def sum_z2():
        t = IPO[2, zh // 2]
        for e in (2, 1, 3):
            arrived(IZ2.at[e - 1], rr.at[2, 4 + e])
            t = t + IZ2[e - 1].astype(F32)
        IXS[...] = t.astype(BF)
        send(IXS, IXR, rs.at[2, 8], rr.at[2, 8], at(dx=2))

    def sum_x(q):
        for n in range(2):
            arrived(IPR.at[n, q], xr.at[n, 15 + q])
        for i in range(2):
            t = IPO[q, i]
            for n in range(2):
                t = t + IPR[n, q, i].astype(F32)
            IZS[q, i] = t.astype(BF)
            IPO[q, i] = t
        for e in (1, 3) if q else (2,):
            send(IZS.at[q, (zh + e) % 4 // 2], IZR.at[e - 1], rs.at[2, e], rr.at[2, e], at(dzh=e))

    def send_zl():
        for i, src, buf in ((0, gate_in, GA), (1, up_in, UP)):
            send(src, buf.at[mine], rs.at[i, 0], rr.at[i, 0], at(dzl=1))

    def input_z():
        for e in (1, 3):
            send(x_in, XF.at[myp, myh], bs.at[1, e, 0], br.at[1, e, 0], at(dzh=e))

    def input_x():
        for d in (1, 3):
            send(x_in, XF.at[myp, myh], bs.at[1, 0, d], br.at[1, 0, d], at(dx=d))

    def gates_here():
        loads[2].wait()
        loads[3].wait()
        for i, buf in ((0, GA), (1, UP)):
            wait_y(i, buf, zl, 0)
            wait_y(i, buf, 1 - zl, 5)

    outs = []

    def weight_grad(i, lhs, rhs, out):
        if i == 0:
            for n in range(4):
                arrived(HID.at[1 - k, pl.ds(base(n), 2)], sr.at[7 + 3 * n])
        if i == 1:
            loads[4].wait()
            wait_x(XF, 1, 2)
        OUT[i] = dot_tn(lhs[...].reshape(16 * T, D), rhs[...].reshape(16 * T, F))
        cp = pltpu.make_async_copy(OUT.at[i], out, osem.at[i])
        cp.start()
        outs.append(cp)

    forward_x(GF, 0, 0)
    forward_z(GF, 0, 1)
    forward_z(GF, 0, 3)
    forward_y(0, GA, zl, 0)
    forward_y(1, UP, zl, 0)
    forward_z(GF, 0, 2)
    send_zl()
    to_sibling(3)
    forward_x(GF, 0, 1)
    forward_x(GF, 0, 3)
    stage_a(3)
    input_x()
    input_z()
    forward_x(GF, 0, 2)
    to_sibling(0)
    to_sibling(1)
    stage_a(0)
    stage_a(1)
    forward_zl(0, GA)
    forward_zl(1, UP)
    to_sibling(2)
    stage_a(2)
    stage_b(0)
    forward_x(XF, 1, 0)
    stage_b(1)
    stage_c(0)
    forward_z(XF, 1, 1)
    forward_z(XF, 1, 3)
    stage_b(2)
    forward_y(0, GA, 1 - zl, 5)
    forward_y(1, UP, 1 - zl, 5)
    stage_c(1)
    stage_d(0)
    forward_z(XF, 1, 2)
    stage_c(2)
    stage_d(1)
    stage_b(3)
    gates_here()
    stage_p(0)
    stage_e(0)
    stage_p(1)
    stage_d(2)
    stage_f(0)
    forward_x(XF, 1, 1)
    forward_x(XF, 1, 3)
    stage_c(3)
    stage_e(1)
    stage_p(2)
    stage_f(1)
    forward_x(XF, 1, 2)
    stage_e(2)
    stage_d(3)
    stage_f(2)
    stage_p(3)
    stage_e(3)
    stage_f(3)
    sum_z2()
    sum_x(1)
    sum_x(0)
    weight_grad(0, GF, HID, gd_out)
    weight_grad(1, XF, DG, gg_out)
    weight_grad(2, XF, DU, gu_out)

    for cp in started:
        cp.wait_send()
    t = IPO[0, zh // 2]
    for e in (1, 2, 3):
        arrived(IZR.at[e - 1], rr.at[2, e])
        t = t + IZR[e - 1].astype(F32)
    arrived(IXR, rr.at[2, 8])
    t = t + IXR[...].astype(F32)
    IGO[...] = t.astype(BF)
    cp = pltpu.make_async_copy(IGO, ig_out, osem.at[3])
    cp.start()
    outs.append(cp)
    for cp in outs:
        cp.wait()


def grads(*args):
    any_spec = pl.BlockSpec(memory_space=pl.ANY)
    dma = pltpu.SemaphoreType.DMA
    return pl.pallas_call(
        kernel,
        out_shape=[
            jax.ShapeDtypeStruct((T, D), BF),
            jax.ShapeDtypeStruct((D, F), F32),
            jax.ShapeDtypeStruct((D, F), F32),
            jax.ShapeDtypeStruct((D, F), F32),
        ],
        in_specs=[any_spec] * 7,
        out_specs=[any_spec] * 4,
        scratch_shapes=[
            pltpu.VMEM((2, 8, T, D), BF),
            pltpu.VMEM((8, T, D), BF),
            pltpu.VMEM((2, 8, T, D), BF),
            pltpu.VMEM((8, T, F), BF),
            pltpu.VMEM((8, T, F), BF),
            pltpu.VMEM((8, T, F), F32),
            pltpu.VMEM((8, T, F), F32),
            pltpu.VMEM((4, 8, Q, F), BF),
            pltpu.VMEM((4, 8, Q, F), F32),
            pltpu.VMEM((4, 7, Q, F), BF),
            pltpu.VMEM((4, Q, F), BF),
            pltpu.VMEM((4, Q, F), BF),
            pltpu.VMEM((8, 4, Q, F), BF),
            pltpu.VMEM((2, 8, T, F), BF),
            pltpu.VMEM((2, 8, T, F), BF),
            pltpu.VMEM((2, 8, T, F), BF),
            pltpu.VMEM((3, 2, T, D), F32),
            pltpu.VMEM((3, 2, 2, T, D), BF),
            pltpu.VMEM((2, 2, 2, T, D), BF),
            pltpu.VMEM((3, T, D), BF),
            pltpu.VMEM((T, D), BF),
            pltpu.VMEM((T, D), BF),
            pltpu.VMEM((2, 2, T, D), BF),
            pltpu.VMEM((3, T, D), BF),
            pltpu.VMEM((D, F), BF),
            pltpu.VMEM((D, F), BF),
            pltpu.VMEM((D, F), BF),
            pltpu.VMEM((D, F), BF),
            pltpu.VMEM((3, D, F), F32),
            pltpu.VMEM((T, D), BF),
            dma((7,)),
            dma((4,)),
            dma((2, 4, 6)),
            dma((2, 4, 6)),
            dma((4, 17)),
            dma((4, 17)),
            dma((3, 10)),
            dma((3, 10)),
            dma((17,)),
            dma((17,)),
        ],
        compiler_params=pltpu.CompilerParams(
            collective_id=0, has_side_effects=True, vmem_limit_bytes=60 * 1024 * 1024
        ),
        cost_estimate=pl.CostEstimate(flops=12 * 2048 * D * F, bytes_accessed=10 << 20, transcendentals=0),
        name="swiglu_backward",
    )(*args)


def hand_over(*refs):
    for src, dst in zip(refs[:4], refs[4:]):
        dst[...] = src[...]


def body(*args):
    outs = grads(*args)
    specs = [pl.BlockSpec((o.shape[0] // 2, o.shape[1]), lambda i: (i, 0)) for o in outs]
    return pl.pallas_call(
        hand_over,
        grid=(2,),
        out_shape=[jax.ShapeDtypeStruct(o.shape, o.dtype) for o in outs],
        in_specs=specs,
        out_specs=specs,
        name="hand_over",
    )(*outs)


def solution(mesh):
    return jax.shard_map(
        body,
        mesh=mesh,
        in_specs=(
            P("col", "row"),
            P("col", "row"),
            P("row", "col"),
            P("row", "col"),
            P("row", "col"),
            P("row", "col"),
            P("row", "col"),
        ),
        out_specs=(P("col", "row"), P("row", "col"), P("row", "col"), P("row", "col")),
        check_vma=False,
    )
```
